32 devices in a mesh: dp: 8 (over y, x, core), tensor: 4 (over z).
Axes of the slice: x: 2, y: 2, z: 4, core: 2. Of those that a mesh axis runs over, the one named last changes fastest.
Arguments:
- activations: bfloat16 [4096, 8192], P('dp'), may hold values from -6 to 6
- cotangent: bfloat16 [4096, 14336], P('dp', 'tensor'), may hold values from -40 to 40
- gate_weight: bfloat16 [8192, 14336], P('dp', 'tensor'), may hold values from -0.046875 to 0.046875
- basis: bfloat16 [8192, 256], replicated, may hold values from -13 to 13
- first_moment: float32 [256, 14336], P('dp', 'tensor'), may hold values from -0.0078125 to 0.0078125
- second_moment: float32 [256, 14336], P('dp', 'tensor'), may hold values from 5e-08 to 1e-06
Outputs:
- input_grad: bfloat16 [4096, 8192], P('dp', 'tensor')
- weight_step: bfloat16 [8192, 14336], P('dp', 'tensor')
- new_first: float32 [256, 14336], P('dp', 'tensor')
- new_second: float32 [256, 14336], P('dp', 'tensor')
The draws below stay inside these ranges and needn't reach their ends.
All inputs are finite; a program needn't handle non-finite values.
Results may differ from the reference program's by a relative error of at most 0.017.
Values may be sent and summed in bfloat16 or wider, within the bound.
A program may use at most 192 MiB of HBM per device.

```python
import math
import jax
import jax.numpy as jnp
from jax import lax

D = 8192
FF = 14336
R = 256
TOKENS = 4096
N_TENSOR = 4


def draw_cotangent(key, part):
    key = jax.random.fold_in(key, 11)
    key_base, key_cols, key_rows = jax.random.split(key, 3)
    base = jnp.clip(jax.random.normal(key_base, (TOKENS, FF), jnp.float32), -4.0, 4.0)
    ramp = 3.0 ** (jnp.arange(FF, dtype=jnp.float32) / FF)
    rough = 10.0 ** jax.random.uniform(key_cols, (FF,), jnp.float32)
    rowscale = 10.0 ** (0.5 * jax.random.uniform(key_rows, (TOKENS, 1), jnp.float32))
    return (base * ramp * rough * rowscale / 10.0).astype(jnp.bfloat16)


def draw_basis(key, part):
    key = jax.random.fold_in(key, 23)
    key_base, key_cols = jax.random.split(key, 2)
    base = jnp.clip(jax.random.normal(key_base, (D, R), jnp.float32), -4.0, 4.0)
    ramp = 3.0 ** (jnp.arange(R, dtype=jnp.float32) / R)
    rough = 10.0 ** (jax.random.uniform(key_cols, (R,), jnp.float32) - 1.0)
    return (base * ramp * rough).astype(jnp.bfloat16)


def steps_of(own_key, shape, cuts, smallest, top_value):
    def one(dim, shards_of):
        draws = jax.random.uniform(jax.random.fold_in(jax.random.fold_in(own_key, 6), dim), (shards_of,), jnp.float32, smallest / len(cuts), top_value / len(cuts))
        return jnp.repeat(jnp.exp(draws), shape[dim] // shards_of).reshape((-1,) + (1,) * (len(shape) - dim - 1))

    factor_of = one(*cuts[0])
    for cut in cuts[1:]:
        factor_of = factor_of * one(*cut)
    return factor_of


def scatter_about(rng, dims, scale, limit, cuts=(), held_as=jnp.bfloat16):
    loudness = steps_of(rng, dims, cuts, -0.22, 0.18) if cuts else 1.0
    drawn = jax.random.normal(rng, dims, jnp.float32) * scale * loudness
    return jnp.minimum(jnp.maximum(drawn, -limit), limit).astype(held_as)


def setup_inputs(seed: int = 0) -> dict:
    key_of = jax.random.split(jax.random.key(seed), 7)
    return {
        "activations": scatter_about(key_of[0], (TOKENS, D), 1.0, 6.0, ((0, 8),)),
        "cotangent": draw_cotangent(jax.random.fold_in(key_of[6], 71), 0),
        "gate_weight": scatter_about(key_of[2], (D, FF), FF ** -0.5, 0.046875, ((0, 8), (1, 4))),
        "basis": draw_basis(jax.random.fold_in(key_of[6], 71), 0),
        "first_moment": scatter_about(key_of[4], (R, FF), 0.0005, 0.0078125, ((0, 8), (1, 4)), jnp.float32),
        "second_moment": jnp.clip(jnp.exp(math.log(9.999999974752427e-07) - 2.9957323 * jax.random.uniform(key_of[5], (R, FF), jnp.float32) ** steps_of(key_of[5], (R, FF), ((0, 8), (1, 4)), -0.2, 0.2)), 5.000000058430487e-08, 9.999999974752427e-07),
    }


beta_one = 0.9
beta_two = 0.999
adam_epsilon = 1e-08
adam_count = 10.0
norm_epsilon = 1e-06

def reference(activations, cotangent, gate_weight, basis, first_moment, second_moment):
    width = FF // N_TENSOR
    summed = jnp.zeros((TOKENS, D), jnp.float32)
    for block in range(N_TENSOR):
        cot_block = cotangent[:, block * width:(block + 1) * width]
        w_block = gate_weight[:, block * width:(block + 1) * width]
        partial_value = lax.dot_general(cot_block, w_block, (((1,), (1,)), ((), ())), preferred_element_type=jnp.float32)
        partial_value = lax.optimization_barrier(partial_value.astype(jnp.bfloat16)).astype(jnp.float32)
        summed = summed + partial_value
    input_grad = summed.astype(jnp.bfloat16)
    coords = jnp.dot(activations, basis, preferred_element_type=jnp.float32).astype(jnp.bfloat16)
    projected = lax.dot_general(coords, cotangent, (((0,), (0,)), ((), ())), preferred_element_type=jnp.float32)
    total = jnp.sum(projected * projected)
    factor = 1.0 / jnp.sqrt(total + norm_epsilon)
    scaled = factor * projected
    new_first = beta_one * first_moment + (1.0 - beta_one) * scaled
    new_second = beta_two * second_moment + (1.0 - beta_two) * scaled * scaled
    first_hat = new_first / (1.0 - beta_one ** adam_count)
    second_hat = new_second / (1.0 - beta_two ** adam_count)
    direction = (first_hat / (jnp.sqrt(second_hat) + adam_epsilon)).astype(jnp.bfloat16)
    weight_step = jnp.dot(basis, direction, preferred_element_type=jnp.float32).astype(jnp.bfloat16)
    return (input_grad, weight_step, new_first, new_second)
```

```python
import functools

import jax
import jax.numpy as jnp
from jax import lax
from jax.sharding import PartitionSpec as P

beta_one = 0.9
beta_two = 0.999
adam_epsilon = 1e-08
adam_count = 10.0
norm_epsilon = 1e-06

x_pieces = 4
early_pieces = 2


def product(left, right):
    return lax.dot_general(
        left, right, (((1,), (1,)), ((), ())), preferred_element_type=jnp.float32
    ).astype(jnp.bfloat16)


def add(left, right):
    return (left.astype(jnp.float32) + right.astype(jnp.float32)).astype(left.dtype)


def on_device(dp_n, z_n, activations, cotangent, gate_weight, basis, first_moment, second_moment):
    high_n = dp_n // 4
    me = lax.axis_index("dp")
    z = lax.axis_index("tensor")
    own_rows = gate_weight.shape[0]

    def swap(value, mask):
        return lax.ppermute(value, "dp", [(i, i ^ mask) for i in range(dp_n)])

    def reduce_block(value, offset):
        for step in range(1, z_n):
            pairs = []
            for i in range(dp_n):
                owner = (i // 2) ^ offset
                if step - 1 < owner:
                    pairs.append((i * z_n + step - 1, i * z_n + step))
                if z_n - step > owner:
                    pairs.append((i * z_n + z_n - step, i * z_n + z_n - step - 1))
            value = add(value, lax.ppermute(value, ("dp", "tensor"), pairs))
        return value

    cot_of = [cotangent] + [swap(cotangent, 4 * h) for h in range(1, high_n)]
    weight_core = swap(gate_weight, 1)

    def both(h, same, other):
        value = jnp.concatenate([product(cot_of[h], same), product(cot_of[h], other)], axis=1)
        return swap(value, 4 * h) if h else value

    reduced = [[] for _ in range(z_n)]
    rows = own_rows // early_pieces
    for h in range(high_n):
        for p in range(early_pieces):
            cut = slice(p * rows, (p + 1) * rows)
            reduced[2 * h].append(
                reduce_block(both(h, gate_weight[cut], weight_core[cut]), 2 * h)
            )
    rows = own_rows // x_pieces
    for p in range(x_pieces):
        same = swap(gate_weight[p * rows : (p + 1) * rows], 2)
        other = swap(same, 1)
        for h in range(high_n):
            reduced[2 * h + 1].append(reduce_block(both(h, same, other), 2 * h + 1))

    def whole(parts):
        half = parts[0].shape[1] // 2
        return jnp.concatenate([v[:, :half] for v in parts] + [v[:, half:] for v in parts], axis=1)

    offset = (me // 2) ^ z
    mine = whole(reduced[0])
    for e in range(1, z_n):
        mine = jnp.where(offset == e, whole(reduced[e]), mine)
    input_grad = jnp.where(me % 2 == 0, mine, jnp.roll(mine, own_rows, axis=1))

    coords = jnp.dot(activations, basis, preferred_element_type=jnp.float32).astype(jnp.bfloat16)
    high_rows = coords.shape[1] // high_n
    owned = 0.0
    for h in range(high_n):
        part = lax.dynamic_slice_in_dim(coords, ((me // 4) ^ h) * high_rows, high_rows, 1)
        part = swap(part, 4 * h) if h else part
        owned = owned + lax.dot_general(
            part, cot_of[h], (((0,), (0,)), ((), ())), preferred_element_type=jnp.float32
        )
    for mask in (2, 1):
        half = owned.shape[0] // 2
        upper = (me & mask) != 0
        keep = jnp.where(upper, owned[half:], owned[:half])
        send = jnp.where(upper, owned[:half], owned[half:]).astype(jnp.bfloat16)
        owned = keep + swap(send, mask).astype(jnp.float32)

    total = jnp.sum(owned * owned).reshape(1, 1)
    mask = 1
    while mask < dp_n:
        total = total + swap(total, mask)
        mask *= 2
    mask = 1
    while mask < z_n:
        total = total + lax.ppermute(total, "tensor", [(i, i ^ mask) for i in range(z_n)])
        mask *= 2
    factor = 1.0 / jnp.sqrt(total + norm_epsilon)
    scaled = factor * owned
    new_first = beta_one * first_moment + (1.0 - beta_one) * scaled
    new_second = beta_two * second_moment + (1.0 - beta_two) * scaled * scaled
    first_hat = new_first / (1.0 - beta_one**adam_count)
    second_hat = new_second / (1.0 - beta_two**adam_count)
    direction = (first_hat / (jnp.sqrt(second_hat) + adam_epsilon)).astype(jnp.bfloat16)
    mask = 1
    while mask < dp_n:
        got = swap(direction, mask)
        upper = (me & mask) != 0
        direction = jnp.concatenate(
            [jnp.where(upper, got, direction), jnp.where(upper, direction, got)], axis=0
        )
        mask *= 2
    basis_rows = lax.dynamic_slice_in_dim(basis, me * own_rows, own_rows, 0)
    weight_step = jnp.dot(
        basis_rows, direction, preferred_element_type=jnp.float32
    ).astype(jnp.bfloat16)
    return (input_grad, weight_step, new_first, new_second)


def solution(mesh):
    dp_n, z_n = mesh.shape["dp"], mesh.shape["tensor"]
    assert dp_n == 2 * z_n and dp_n % 4 == 0
    in_specs = (
        P("dp", None),
        P("dp", "tensor"),
        P("dp", "tensor"),
        P(),
        P("dp", "tensor"),
        P("dp", "tensor"),
    )
    out_specs = (P("dp", "tensor"), P("dp", "tensor"), P("dp", "tensor"), P("dp", "tensor"))
    return jax.shard_map(
        functools.partial(on_device, dp_n, z_n),
        mesh=mesh,
        in_specs=in_specs,
        out_specs=out_specs,
        check_vma=False,
    )
```

```python
import functools

import jax
import jax.numpy as jnp
from jax import lax
from jax.experimental import pallas as pl
from jax.experimental.pallas import tpu as pltpu
from jax.sharding import PartitionSpec as P

beta_one = 0.9
beta_two = 0.999
adam_epsilon = 1e-08
adam_count = 10.0
norm_epsilon = 1e-06

x_pieces = 4
early_pieces = 2


def product(left, right):
    return lax.dot_general(
        left, right, (((1,), (1,)), ((), ())), preferred_element_type=jnp.float32
    ).astype(jnp.bfloat16)


def add(left, right):
    return (left.astype(jnp.float32) + right.astype(jnp.float32)).astype(left.dtype)


def on_device(dp_n, z_n, activations, cotangent, gate_weight, basis, first_moment, second_moment):
    high_n = dp_n // 4
    me = lax.axis_index("dp")
    z = lax.axis_index("tensor")
    own_rows = gate_weight.shape[0]

    def swap(value, mask):
        return lax.ppermute(value, "dp", [(i, i ^ mask) for i in range(dp_n)])

    def reduce_block(value, offset):
        for step in range(1, z_n):
            pairs = []
            for i in range(dp_n):
                owner = (i // 2) ^ offset
                if step - 1 < owner:
                    pairs.append((i * z_n + step - 1, i * z_n + step))
                if z_n - step > owner:
                    pairs.append((i * z_n + z_n - step, i * z_n + z_n - step - 1))
            value = add(value, lax.ppermute(value, ("dp", "tensor"), pairs))
        return value

    cot_of = [cotangent] + [swap(cotangent, 4 * h) for h in range(1, high_n)]
    weight_core = swap(gate_weight, 1)

    def both(h, same, other):
        value = jnp.concatenate([product(cot_of[h], same), product(cot_of[h], other)], axis=1)
        return swap(value, 4 * h) if h else value

    reduced = [[] for _ in range(z_n)]
    rows = own_rows // early_pieces
    for h in range(high_n):
        for p in range(early_pieces):
            cut = slice(p * rows, (p + 1) * rows)
            reduced[2 * h].append(
                reduce_block(both(h, gate_weight[cut], weight_core[cut]), 2 * h)
            )
    rows = own_rows // x_pieces
    for p in range(x_pieces):
        same = swap(gate_weight[p * rows : (p + 1) * rows], 2)
        other = swap(same, 1)
        for h in range(high_n):
            reduced[2 * h + 1].append(reduce_block(both(h, same, other), 2 * h + 1))

    def whole(parts):
        half = parts[0].shape[1] // 2
        return jnp.concatenate([v[:, :half] for v in parts] + [v[:, half:] for v in parts], axis=1)

    offset = (me // 2) ^ z
    mine = whole(reduced[0])
    for e in range(1, z_n):
        mine = jnp.where(offset == e, whole(reduced[e]), mine)
    input_grad = jnp.where(me % 2 == 0, mine, jnp.roll(mine, own_rows, axis=1))

    coords = jnp.dot(activations, basis, preferred_element_type=jnp.float32).astype(jnp.bfloat16)
    high_rows = coords.shape[1] // high_n
    owned = 0.0
    for h in range(high_n):
        part = lax.dynamic_slice_in_dim(coords, ((me // 4) ^ h) * high_rows, high_rows, 1)
        part = swap(part, 4 * h) if h else part
        owned = owned + lax.dot_general(
            part, cot_of[h], (((0,), (0,)), ((), ())), preferred_element_type=jnp.float32
        )
    for mask in (2, 1):
        half = owned.shape[0] // 2
        upper = (me & mask) != 0
        keep = jnp.where(upper, owned[half:], owned[:half])
        send = jnp.where(upper, owned[:half], owned[half:]).astype(jnp.bfloat16)
        owned = keep + swap(send, mask).astype(jnp.float32)

    total = jnp.sum(owned * owned).reshape(1, 1)
    mask = 1
    while mask < dp_n:
        total = total + swap(total, mask)
        mask *= 2
    mask = 1
    while mask < z_n:
        total = total + lax.ppermute(total, "tensor", [(i, i ^ mask) for i in range(z_n)])
        mask *= 2
    factor = 1.0 / jnp.sqrt(total + norm_epsilon)
    scaled = factor * owned
    new_first = beta_one * first_moment + (1.0 - beta_one) * scaled
    new_second = beta_two * second_moment + (1.0 - beta_two) * scaled * scaled
    first_hat = new_first / (1.0 - beta_one**adam_count)
    second_hat = new_second / (1.0 - beta_two**adam_count)
    direction = (first_hat / (jnp.sqrt(second_hat) + adam_epsilon)).astype(jnp.bfloat16)
    mask = 1
    while mask < dp_n:
        got = swap(direction, mask)
        upper = (me & mask) != 0
        direction = jnp.concatenate(
            [jnp.where(upper, got, direction), jnp.where(upper, direction, got)], axis=0
        )
        mask *= 2
    basis_rows = lax.dynamic_slice_in_dim(basis, me * own_rows, own_rows, 0)
    weight_step = jnp.dot(
        basis_rows, direction, preferred_element_type=jnp.float32
    ).astype(jnp.bfloat16)
    return (input_grad, weight_step, new_first, new_second)


def moments(factor, owned, first, second):
    scaled = factor * owned
    new_first = beta_one * first + (1.0 - beta_one) * scaled
    new_second = beta_two * second + (1.0 - beta_two) * scaled * scaled
    first_hat = new_first / (1.0 - beta_one**adam_count)
    second_hat = new_second / (1.0 - beta_two**adam_count)
    direction = (first_hat / (jnp.sqrt(second_hat) + adam_epsilon)).astype(jnp.bfloat16)
    return new_first, new_second, direction


ORDER = (
    (0, 0), (0, 1), (0, 2), (0, 3), (1, 0), (1, 1), (2, 0), (2, 1),
    (2, 2), (1, 2), (2, 3), (3, 0), (3, 1), (1, 3), (3, 2), (3, 3),
)
CHUNKS = 4
LAG = 2


def exchange_kernel(
    z_n, cot_ref, w_ref, coords_ref, first_ref, second_ref,
    grad_ref, new_first_ref, new_second_ref, dirs_out_ref,
    cots, ws, parts, z_got, fin_got, coords_got, proj, proj_send, proj_got, sums, zsums, dirs,
    local_sem, cot_send, cot_recv, w_send, w_recv, ret_send, ret_recv, z_send, z_recv,
    fin_send, fin_recv, co_send, co_recv, px_send, px_recv, s_send, s_recv, t_send, t_recv,
    d_send, d_recv,
):
    me = lax.axis_index("dp")
    z = lax.axis_index("tensor")
    core = me % 2
    x_bit = (me // 2) % 2
    y_bit = me // 4
    block = me // 2
    tokens = cots.shape[1]
    cols = parts.shape[3]
    half_tokens = tokens // 2

    def flip(mask):
        c = 1 - core if mask & 1 else core
        x = 1 - x_bit if mask & 2 else x_bit
        y = 1 - y_bit if mask & 4 else y_bit
        return y * 4 + x * 2 + c

    def remote(src, dst, send, recv, dp, tensor):
        return pltpu.make_async_remote_copy(
            src_ref=src, dst_ref=dst, send_sem=send, recv_sem=recv,
            device_id=(dp, tensor), device_id_type=pl.DeviceIdType.MESH,
        )

    barrier = pltpu.get_barrier_semaphore()
    for mask in range(1, 8):
        pl.semaphore_signal(barrier, inc=1, device_id=(flip(mask), z), device_id_type=pl.DeviceIdType.MESH)
    for step in range(1, z_n):
        pl.semaphore_signal(barrier, inc=1, device_id=(me, (z + step) % z_n), device_id_type=pl.DeviceIdType.MESH)
    local = [
        pltpu.make_async_copy(cot_ref, cots.at[0], local_sem.at[0]),
        pltpu.make_async_copy(w_ref, ws.at[0], local_sem.at[1]),
    ]
    for copy in local:
        copy.start()
    pl.semaphore_wait(barrier, 7 + z_n - 1)

    def w_copy(p):
        rows = pl.ds(p * cols, cols)
        return remote(w_ref.at[rows], ws.at[1, rows], w_send.at[p], w_recv.at[p], flip(2), z)

    def y_copy(h):
        rows = pl.ds(h * half_tokens, half_tokens)
        return remote(cot_ref.at[rows], cots.at[2, rows], cot_send.at[1 + h], cot_recv.at[1 + h], flip(4), z)

    def forward_copy(h):
        rows = pl.ds(h * half_tokens, half_tokens)
        return remote(cots.at[2, rows], cots.at[3, rows], cot_send.at[3 + h], cot_recv.at[3 + h], flip(1), z)

    core_copy = remote(cot_ref, cots.at[1], cot_send.at[0], cot_recv.at[0], flip(1), z)

    high_rows = coords_ref.shape[0] // 4

    def coords_rows(b):
        return coords_ref.at[pl.ds(pl.multiple_of(b * high_rows, high_rows), high_rows)]

    def coords_copy(m):
        mask = (m & 1) + 2 * (m & 2)
        there = flip(mask)
        b = (there // 4) * 2 + there % 2
        return remote(coords_rows(b), coords_got.at[m - 1], co_send.at[m - 1], co_recv.at[m - 1], there, z)

    w_copy(0).start()
    y_copy(0).start()
    core_copy.start()
    for m in range(1, 4):
        coords_copy(m).start()
    w_copy(1).start()
    y_copy(1).start()
    for copy in local:
        copy.wait()

    def unit(t, w, q):
        value = lax.dot_general(
            cots[t], ws[w, pl.ds(pl.multiple_of(q * cols, cols), cols), :],
            (((1,), (1,)), ((), ())), preferred_element_type=jnp.float32,
        )
        rows = pl.ds(pl.multiple_of((t % 2) * tokens, tokens), tokens)
        parts[w + 4 * (t // 2), q, rows, :] = value.astype(jnp.bfloat16)

    def return_copy(w, q):
        i = w * CHUNKS + q
        return remote(parts.at[4 + w, q], parts.at[2 + w, q], ret_send.at[i], ret_recv.at[i], flip(4), z)

    def owner(e):
        y = 1 - y_bit if e & 2 else y_bit
        x = 1 - x_bit if e & 1 else x_bit
        return y * 2 + x

    def accumulate(e, q, slots):
        def body(i, carry):
            rows = pl.ds(pl.multiple_of(i * 64, 64), 64)
            value = parts[e, q, rows, :].astype(jnp.float32)
            for slot in slots:
                value = value + z_got[slot, q, rows, :].astype(jnp.float32)
            parts[e, q, rows, :] = value.astype(jnp.bfloat16)
            return carry
        lax.fori_loop(0, 2 * tokens // 64, body, 0)

    def right_copy(e, q):
        s = owner(e)
        return remote(parts.at[e, q], z_got.at[s + 1, q], z_send.at[e, q], z_recv.at[s + 1, q], me, lax.rem(z + 1, z_n))

    def left_copy(e, q):
        s = owner(e)
        return remote(parts.at[e, q], z_got.at[s, q], z_send.at[e, q], z_recv.at[s, q], me, lax.rem(z + z_n - 1, z_n))

    def z_round(e, q, k):
        s = owner(e)
        if k < z_n:
            @pl.when((z == k - 1) & (z < s))
            def _():
                if k > 1:
                    right_copy(e, q).wait_recv()
                    accumulate(e, q, [s + 1])
                right_copy(e, q).start()

            @pl.when((z == z_n - k) & (z > s))
            def _():
                if k > 1:
                    left_copy(e, q).wait_recv()
                    accumulate(e, q, [s])
                left_copy(e, q).start()
        else:
            @pl.when(z == s)
            def _():
                @pl.when(z > 0)
                def _():
                    right_copy(e, q).wait_recv()
                    accumulate(e, q, [s + 1])

                @pl.when(z < z_n - 1)
                def _():
                    left_copy(e, q).wait_recv()
                    accumulate(e, q, [s])
                fin_copy(e, q).start()
                grad_ref[:, pl.ds(pl.multiple_of((core * CHUNKS + q) * cols, cols), cols)] = parts[e, q, :tokens, :]

    def fin_copy(e, q):
        return remote(parts.at[e, q, pl.ds(tokens, tokens)], fin_got.at[q], fin_send.at[q], fin_recv.at[q], flip(1), z)

    def two_units(base, w, q):
        def body(t, carry):
            unit(base + t, w, q)
            return carry
        lax.fori_loop(0, 2, body, 0)

    def project():
        b = y_bit * 2 + core
        own = pl.ds(pl.multiple_of(b * high_rows, high_rows), high_rows)
        width = cols
        def body(i, carry):
            at = pl.ds(pl.multiple_of(i * width, width), width)
            value = jnp.dot(coords_ref[own, :], cots[0, :, at], preferred_element_type=jnp.float32)
            for m in range(1, 4):
                value = value + jnp.dot(coords_got[m - 1], cots[m, :, at], preferred_element_type=jnp.float32)
            proj[:, at] = value
            return carry
        lax.fori_loop(0, proj.shape[1] // width, body, 0)

    out_rows = proj.shape[0] // 2
    proj_copy = remote(proj_send, proj_got, px_send, px_recv, flip(2), z)

    def send_projected():
        project()
        there = pl.ds(pl.multiple_of((1 - x_bit) * out_rows, out_rows), out_rows)
        proj_send[...] = proj[there, :].astype(jnp.bfloat16)
        proj_copy.start()

    def sum_copy(m):
        return remote(sums.at[0], sums.at[m], s_send.at[m], s_recv.at[m], flip(m), z)

    def zsum_copy(step):
        return remote(zsums.at[0], zsums.at[step], t_send.at[step], t_recv.at[step], me, (z + step) % z_n)

    here = pl.ds(pl.multiple_of(x_bit * out_rows, out_rows), out_rows)

    def send_sums():
        proj_copy.wait()
        owned = proj[here, :] + proj_got[...].astype(jnp.float32)
        proj[here, :] = owned
        sums[0] = jnp.zeros((8, 128), jnp.float32) + jnp.sum(owned * owned)
        for m in range(1, 8):
            sum_copy(m).start()

    def send_zsums():
        for m in range(1, 8):
            sum_copy(m).wait()
        zsums[0] = jnp.sum(sums[...], axis=0)
        for step in range(1, z_n):
            zsum_copy(step).start()

    def dir_copy(m):
        return remote(dirs.at[me], dirs.at[me], d_send.at[m], d_recv.at[m], flip(m), z)

    def send_dirs():
        for step in range(1, z_n):
            zsum_copy(step).wait()
        total = jnp.sum(zsums[...], axis=0)
        factor = (1.0 / jnp.sqrt(total + norm_epsilon))[0:1, 0:1]
        one, two, direction = moments(factor, proj[here, :], first_ref[...], second_ref[...])
        new_first_ref[...] = one
        new_second_ref[...] = two
        dirs[me] = direction
        for m in range(1, 8):
            dir_copy(m).start()

    def take_dirs():
        for m in range(1, 8):
            dir_copy(m).wait()
        dirs_out_ref[...] = dirs[...].reshape(dirs_out_ref.shape)

    def before(i):
        e, q = ORDER[i]
        if i == 0:
            def body(j, carry):
                unit(0, 0, j)
                return carry
            lax.fori_loop(0, CHUNKS, body, 0)
            core_copy.wait()
        if e == 0:
            unit(1, 0, q)
        if e == 1:
            w_copy(q).wait()
            if q + 2 < CHUNKS:
                w_copy(q + 2).start()
            two_units(0, 1, q)
        if e >= 2:
            return_copy(e - 2, q).wait()

    def after(i):
        e, q = ORDER[i]
        if (e, q) == (1, 0):
            y_copy(0).wait()
            forward_copy(0).start()
        if (e, q) == (1, 1):
            y_copy(1).wait()
            forward_copy(1).start()
            for h in range(2):
                forward_copy(h).wait_recv()
            for w, p in ((0, 0), (0, 1), (0, 2), (0, 3), (1, 0), (1, 1)):
                two_units(2, w, p)
                return_copy(w, p).start()
                if (w, p) == (0, 0):
                    for m in range(1, 4):
                        coords_copy(m).wait()
                    send_projected()
        if e == 1 and q >= 2:
            two_units(2, 1, q)
            return_copy(1, q).start()

    stages = {8: send_sums, 10: send_zsums, 12: send_dirs}
    count = len(ORDER)
    for i in range(count + LAG * (z_n - 1)):
        if i < count:
            before(i)
            z_round(*ORDER[i], 1)
            after(i)
        for k in range(2, z_n + 1):
            j = i - LAG * (k - 1)
            if 0 <= j < count:
                z_round(*ORDER[j], k)
        if i in stages:
            stages[i]()
    take_dirs()
    for q in range(CHUNKS):
        fin_copy(0, q).wait()
        grad_ref[:, pl.ds(pl.multiple_of(((1 - core) * CHUNKS + q) * cols, cols), cols)] = fin_got[q]
    for h in range(2):
        forward_copy(h).wait_send()
    for e, q in ORDER:
        @pl.when(z != owner(e))
        def _():
            right_copy(e, q).wait_send()


def exchange(z_n, cotangent, gate_weight, coords, first_moment, second_moment):
    tokens, hidden = cotangent.shape
    w_rows = gate_weight.shape[0]
    cols = w_rows // CHUNKS
    rank = coords.shape[0]
    own = first_moment.shape[0]
    vmem = pl.BlockSpec(memory_space=pltpu.VMEM)
    hbm = pl.BlockSpec(memory_space=pl.ANY)
    dma = pltpu.SemaphoreType.DMA
    bf16, f32 = jnp.bfloat16, jnp.float32
    flops = 2 * 4 * tokens * 2 * w_rows * hidden
    return pl.pallas_call(
        functools.partial(exchange_kernel, z_n),
        out_shape=[
            jax.ShapeDtypeStruct((tokens, 2 * w_rows), bf16),
            jax.ShapeDtypeStruct(first_moment.shape, f32),
            jax.ShapeDtypeStruct(first_moment.shape, f32),
            jax.ShapeDtypeStruct((rank, hidden), bf16),
        ],
        in_specs=[hbm, hbm, vmem, vmem, vmem],
        out_specs=[vmem] * 4,
        scratch_shapes=[
            pltpu.VMEM((4, tokens, hidden), bf16),
            pltpu.VMEM((2, w_rows, hidden), bf16),
            pltpu.VMEM((6, CHUNKS, 2 * tokens, cols), bf16),
            pltpu.VMEM((z_n + 1, CHUNKS, 2 * tokens, cols), bf16),
            pltpu.VMEM((CHUNKS, tokens, cols), bf16),
            pltpu.VMEM((3, rank // 4, tokens), bf16),
            pltpu.VMEM((2 * own, hidden), f32),
            pltpu.VMEM((own, hidden), bf16),
            pltpu.VMEM((own, hidden), bf16),
            pltpu.VMEM((8, 8, 128), f32),
            pltpu.VMEM((z_n, 8, 128), f32),
            pltpu.VMEM((8, own, hidden), bf16),
            dma((2,)),
            dma((5,)), dma((5,)),
            dma((CHUNKS,)), dma((CHUNKS,)),
            dma((2 * CHUNKS,)), dma((2 * CHUNKS,)),
            dma((4, CHUNKS)), dma((z_n + 1, CHUNKS)),
            dma((CHUNKS,)), dma((CHUNKS,)),
            dma((3,)), dma((3,)),
            dma, dma,
            dma((8,)), dma((8,)),
            dma((z_n,)), dma((z_n,)),
            dma((8,)), dma((8,)),
        ],
        compiler_params=pltpu.CompilerParams(
            collective_id=0, has_side_effects=True, vmem_limit_bytes=62 * 1024 * 1024
        ),
        cost_estimate=pl.CostEstimate(flops=flops, bytes_accessed=24000000, transcendentals=0),
    )(cotangent, gate_weight, coords, first_moment, second_moment)


def on_pairs(z_n, activations, cotangent, gate_weight, basis, first_moment, second_moment):
    own_rows = gate_weight.shape[0]
    tokens = activations.shape[0]
    rank = basis.shape[1]
    me = lax.axis_index("dp")
    coords = lax.dot_general(
        basis, activations, (((0,), (1,)), ((), ())), preferred_element_type=jnp.float32
    ).astype(jnp.bfloat16)
    coords = coords.reshape(2, 2, 2, rank // 8, tokens).transpose(0, 2, 1, 3, 4).reshape(rank, tokens)
    input_grad, new_first, new_second, direction = exchange(
        z_n, cotangent, gate_weight, coords, first_moment, second_moment
    )
    basis_rows = lax.dynamic_slice_in_dim(basis, me * own_rows, own_rows, 0)
    weight_step = jnp.dot(
        basis_rows, direction, preferred_element_type=jnp.float32
    ).astype(jnp.bfloat16)
    return (input_grad, weight_step, new_first, new_second)


def solution(mesh):
    dp_n, z_n = mesh.shape["dp"], mesh.shape["tensor"]
    assert dp_n == 2 * z_n and dp_n % 4 == 0
    paired = (dp_n, z_n) == (8, 4)
    body = functools.partial(on_pairs, z_n) if paired else functools.partial(on_device, dp_n, z_n)
    in_specs = (
        P("dp", None),
        P("dp", "tensor"),
        P("dp", "tensor"),
        P(),
        P("dp", "tensor"),
        P("dp", "tensor"),
    )
    out_specs = (P("dp", "tensor"), P("dp", "tensor"), P("dp", "tensor"), P("dp", "tensor"))
    return jax.shard_map(
        body,
        mesh=mesh,
        in_specs=in_specs,
        out_specs=out_specs,
        check_vma=False,
    )
```

```python
import functools

import jax
import jax.numpy as jnp
from jax import lax
from jax.experimental import pallas as pl
from jax.experimental.pallas import tpu as pltpu
from jax.sharding import PartitionSpec as P

beta_one = 0.9
beta_two = 0.999
adam_epsilon = 1e-08
adam_count = 10.0
norm_epsilon = 1e-06

x_pieces = 4
early_pieces = 2


def product(left, right):
    return lax.dot_general(
        left, right, (((1,), (1,)), ((), ())), preferred_element_type=jnp.float32
    ).astype(jnp.bfloat16)


def add(left, right):
    return (left.astype(jnp.float32) + right.astype(jnp.float32)).astype(left.dtype)


def on_device(dp_n, z_n, activations, cotangent, gate_weight, basis, first_moment, second_moment):
    high_n = dp_n // 4
    me = lax.axis_index("dp")
    z = lax.axis_index("tensor")
    own_rows = gate_weight.shape[0]

    def swap(value, mask):
        return lax.ppermute(value, "dp", [(i, i ^ mask) for i in range(dp_n)])

    def reduce_block(value, offset):
        for step in range(1, z_n):
            pairs = []
            for i in range(dp_n):
                owner = (i // 2) ^ offset
                if step - 1 < owner:
                    pairs.append((i * z_n + step - 1, i * z_n + step))
                if z_n - step > owner:
                    pairs.append((i * z_n + z_n - step, i * z_n + z_n - step - 1))
            value = add(value, lax.ppermute(value, ("dp", "tensor"), pairs))
        return value

    cot_of = [cotangent] + [swap(cotangent, 4 * h) for h in range(1, high_n)]
    weight_core = swap(gate_weight, 1)

    def both(h, same, other):
        value = jnp.concatenate([product(cot_of[h], same), product(cot_of[h], other)], axis=1)
        return swap(value, 4 * h) if h else value

    reduced = [[] for _ in range(z_n)]
    rows = own_rows // early_pieces
    for h in range(high_n):
        for p in range(early_pieces):
            cut = slice(p * rows, (p + 1) * rows)
            reduced[2 * h].append(
                reduce_block(both(h, gate_weight[cut], weight_core[cut]), 2 * h)
            )
    rows = own_rows // x_pieces
    for p in range(x_pieces):
        same = swap(gate_weight[p * rows : (p + 1) * rows], 2)
        other = swap(same, 1)
        for h in range(high_n):
            reduced[2 * h + 1].append(reduce_block(both(h, same, other), 2 * h + 1))

    def whole(parts):
        half = parts[0].shape[1] // 2
        return jnp.concatenate([v[:, :half] for v in parts] + [v[:, half:] for v in parts], axis=1)

    offset = (me // 2) ^ z
    mine = whole(reduced[0])
    for e in range(1, z_n):
        mine = jnp.where(offset == e, whole(reduced[e]), mine)
    input_grad = jnp.where(me % 2 == 0, mine, jnp.roll(mine, own_rows, axis=1))

    coords = jnp.dot(activations, basis, preferred_element_type=jnp.float32).astype(jnp.bfloat16)
    high_rows = coords.shape[1] // high_n
    owned = 0.0
    for h in range(high_n):
        part = lax.dynamic_slice_in_dim(coords, ((me // 4) ^ h) * high_rows, high_rows, 1)
        part = swap(part, 4 * h) if h else part
        owned = owned + lax.dot_general(
            part, cot_of[h], (((0,), (0,)), ((), ())), preferred_element_type=jnp.float32
        )
    for mask in (2, 1):
        half = owned.shape[0] // 2
        upper = (me & mask) != 0
        keep = jnp.where(upper, owned[half:], owned[:half])
        send = jnp.where(upper, owned[:half], owned[half:]).astype(jnp.bfloat16)
        owned = keep + swap(send, mask).astype(jnp.float32)

    total = jnp.sum(owned * owned).reshape(1, 1)
    mask = 1
    while mask < dp_n:
        total = total + swap(total, mask)
        mask *= 2
    mask = 1
    while mask < z_n:
        total = total + lax.ppermute(total, "tensor", [(i, i ^ mask) for i in range(z_n)])
        mask *= 2
    factor = 1.0 / jnp.sqrt(total + norm_epsilon)
    scaled = factor * owned
    new_first = beta_one * first_moment + (1.0 - beta_one) * scaled
    new_second = beta_two * second_moment + (1.0 - beta_two) * scaled * scaled
    first_hat = new_first / (1.0 - beta_one**adam_count)
    second_hat = new_second / (1.0 - beta_two**adam_count)
    direction = (first_hat / (jnp.sqrt(second_hat) + adam_epsilon)).astype(jnp.bfloat16)
    mask = 1
    while mask < dp_n:
        got = swap(direction, mask)
        upper = (me & mask) != 0
        direction = jnp.concatenate(
            [jnp.where(upper, got, direction), jnp.where(upper, direction, got)], axis=0
        )
        mask *= 2
    basis_rows = lax.dynamic_slice_in_dim(basis, me * own_rows, own_rows, 0)
    weight_step = jnp.dot(
        basis_rows, direction, preferred_element_type=jnp.float32
    ).astype(jnp.bfloat16)
    return (input_grad, weight_step, new_first, new_second)


def moments(factor, owned, first, second):
    scaled = factor * owned
    new_first = beta_one * first + (1.0 - beta_one) * scaled
    new_second = beta_two * second + (1.0 - beta_two) * scaled * scaled
    first_hat = new_first / (1.0 - beta_one**adam_count)
    second_hat = new_second / (1.0 - beta_two**adam_count)
    direction = (first_hat / (jnp.sqrt(second_hat) + adam_epsilon)).astype(jnp.bfloat16)
    return new_first, new_second, direction


START, OWN, X, Y, BACK, Z, PROJECT, SUMS, ZSUMS, DIRS = range(10)
ORDER = (
    (START,), (OWN, 0), (OWN, 1), (Z, 0, 1, 0, 1), (Z, 0, 0, 0, 1),
    (Z, 0, 0, 0, 2), (Y, 0), (OWN, 2), (OWN, 3), (Z, 0, 3, 0, 1),
    (BACK, 2, 2, 0), (Z, 0, 3, 0, 2), (Z, 0, 3, 0, 3), (X, 0), (Z, 1, 0, 0, 1),
    (BACK, 2, 0, 0), (BACK, 2, 1, 0), (Z, 0, 1, 0, 2), (BACK, 2, 3, 0), (Y, 1),
    (Z, 0, 0, 0, 3), (Z, 0, 2, 0, 1), (X, 1), (Z, 1, 1, 0, 1), (Z, 0, 2, 0, 2),
    (Z, 2, 2, 0, 1), (BACK, 3, 0, 0), (Z, 2, 0, 0, 1), (Z, 2, 0, 0, 2), (BACK, 3, 1, 0),
    (Z, 0, 1, 0, 3), (Z, 1, 1, 0, 2), (Z, 0, 3, 0, 4), (Z, 2, 1, 0, 1), (BACK, 2, 2, 1),
    (Z, 0, 2, 0, 3), (Z, 2, 1, 0, 2), (BACK, 2, 0, 1), (PROJECT,), (Z, 1, 1, 0, 3),
    (Z, 2, 3, 0, 1), (BACK, 3, 1, 1), (Z, 3, 0, 0, 1), (BACK, 2, 1, 1), (BACK, 3, 0, 1),
    (Z, 2, 0, 0, 3), (Z, 3, 1, 0, 1), (Z, 3, 1, 0, 2), (X, 2), (BACK, 3, 2, 0),
    (Z, 1, 2, 0, 1), (BACK, 3, 2, 1), (Z, 3, 0, 0, 2), (Z, 2, 2, 0, 2), (Z, 1, 0, 0, 2),
    (BACK, 2, 3, 1), (Z, 2, 0, 0, 4), (Z, 2, 2, 1, 1), (Z, 2, 2, 1, 2), (Z, 1, 0, 0, 3),
    (Z, 2, 2, 1, 3), (Z, 3, 1, 1, 1), (Z, 2, 1, 1, 1), (Z, 3, 1, 1, 2), (Z, 2, 0, 1, 1),
    (Z, 0, 0, 0, 4), (Z, 2, 1, 1, 2), (Z, 3, 2, 1, 1), (Z, 3, 2, 0, 1), (Z, 2, 3, 1, 1),
    (Z, 3, 2, 1, 2), (Z, 0, 1, 0, 4), (SUMS,), (Z, 1, 1, 0, 4), (Z, 0, 2, 0, 4),
    (Z, 3, 2, 0, 2), (Z, 2, 0, 1, 2), (Z, 1, 2, 0, 2), (X, 3), (BACK, 3, 3, 0),
    (Z, 3, 1, 1, 3), (Z, 2, 1, 0, 3), (Z, 2, 0, 1, 3), (BACK, 3, 3, 1), (Z, 3, 0, 0, 3),
    (Z, 1, 3, 0, 1), (Z, 3, 2, 0, 3), (Z, 2, 3, 0, 2), (Z, 2, 2, 0, 3), (Z, 2, 2, 1, 4),
    (ZSUMS,), (Z, 1, 3, 0, 2), (Z, 3, 1, 1, 4), (Z, 2, 3, 1, 2), (Z, 2, 3, 1, 3),
    (Z, 3, 3, 0, 1), (Z, 3, 3, 0, 2), (Z, 2, 1, 1, 3), (Z, 3, 1, 0, 3), (Z, 3, 3, 1, 1),
    (Z, 3, 0, 0, 4), (Z, 1, 2, 0, 3), (DIRS,), (Z, 3, 3, 1, 2), (Z, 3, 2, 1, 3),
    (Z, 2, 3, 1, 4), (Z, 3, 2, 1, 4), (Z, 3, 1, 0, 4), (Z, 3, 2, 0, 4), (Z, 2, 2, 0, 4),
    (Z, 3, 3, 0, 3), (Z, 3, 0, 1, 1), (Z, 2, 1, 0, 4), (Z, 3, 0, 1, 2), (Z, 1, 2, 0, 4),
    (Z, 1, 3, 0, 3), (Z, 3, 3, 1, 3), (Z, 2, 1, 1, 4), (Z, 3, 3, 0, 4), (Z, 2, 0, 1, 4),
    (Z, 2, 3, 0, 3), (Z, 3, 3, 1, 4), (Z, 1, 3, 0, 4), (Z, 3, 0, 1, 3), (Z, 3, 0, 1, 4),
    (Z, 2, 3, 0, 4), (Z, 1, 0, 0, 4),
)
CHUNKS = 4
AHEAD = 3


def exchange_kernel(
    z_n, cot_ref, w_ref, coords_ref, first_ref, second_ref,
    grad_ref, new_first_ref, new_second_ref, dirs_out_ref,
    cots, ws, parts, z_got, fin_got, coords_got, proj, proj_send, proj_got, sums, zsums, dirs,
    local_sem, cot_send, cot_recv, w_send, w_recv, ret_send, ret_recv, z_send, z_recv,
    fin_send, fin_recv, co_send, co_recv, px_send, px_recv, s_send, s_recv, t_send, t_recv,
    d_send, d_recv,
):
    me = lax.axis_index("dp")
    z = lax.axis_index("tensor")
    core = me % 2
    x_bit = (me // 2) % 2
    y_bit = me // 4
    block = me // 2
    half = cots.shape[1] // 2
    cols = parts.shape[4]

    def flip(mask):
        c = 1 - core if mask & 1 else core
        x = 1 - x_bit if mask & 2 else x_bit
        y = 1 - y_bit if mask & 4 else y_bit
        return y * 4 + x * 2 + c

    def remote(src, dst, send, recv, dp, tensor):
        return pltpu.make_async_remote_copy(
            src_ref=src, dst_ref=dst, send_sem=send, recv_sem=recv,
            device_id=(dp, tensor), device_id_type=pl.DeviceIdType.MESH,
        )

    barrier = pltpu.get_barrier_semaphore()
    for mask in range(1, 8):
        pl.semaphore_signal(barrier, inc=1, device_id=(flip(mask), z), device_id_type=pl.DeviceIdType.MESH)
    for step in range(1, z_n):
        pl.semaphore_signal(barrier, inc=1, device_id=(me, (z + step) % z_n), device_id_type=pl.DeviceIdType.MESH)
    local = [
        pltpu.make_async_copy(cot_ref.at[pl.ds(0, half)], cots.at[0, pl.ds(0, half)], local_sem.at[0]),
        pltpu.make_async_copy(cot_ref.at[pl.ds(half, half)], cots.at[1, pl.ds(0, half)], local_sem.at[1]),
        pltpu.make_async_copy(w_ref, ws.at[0], local_sem.at[2]),
    ]
    for copy in local:
        copy.start()
    pl.semaphore_wait(barrier, 7 + z_n - 1)

    def w_copy(p):
        rows = pl.ds(p * cols, cols)
        return remote(w_ref.at[rows], ws.at[1, rows], w_send.at[p], w_recv.at[p], flip(2), z)

    def y_copy(h):
        rows = pl.ds(h * half, half)
        return remote(cot_ref.at[rows], cots.at[2 + h, pl.ds(0, half)], cot_send.at[2 + h], cot_recv.at[2 + h], flip(4), z)

    def forward_copy(h):
        return remote(cots.at[2 + h, pl.ds(0, half)], cots.at[2 + h, pl.ds(half, half)], cot_send.at[4 + h], cot_recv.at[4 + h], flip(1), z)

    def core_copy(h):
        rows = pl.ds(h * half, half)
        return remote(cot_ref.at[rows], cots.at[h, pl.ds(half, half)], cot_send.at[h], cot_recv.at[h], flip(1), z)

    high_rows = coords_ref.shape[0] // 4

    def coords_rows(b):
        return coords_ref.at[pl.ds(pl.multiple_of(b * high_rows, high_rows), high_rows)]

    def coords_copy(m):
        mask = (m & 1) + 2 * (m & 2)
        there = flip(mask)
        b = (there // 4) * 2 + there % 2
        return remote(coords_rows(b), coords_got.at[m - 1], co_send.at[m - 1], co_recv.at[m - 1], there, z)

    w_copy(0).start()
    y_copy(0).start()
    for h in range(2):
        core_copy(h).start()
    for m in range(1, 4):
        coords_copy(m).start()
    for p in range(1, AHEAD):
        w_copy(p).start()
    for copy in local:
        copy.wait()

    def unit(g, w, q):
        value = lax.dot_general(
            cots[g], ws[w, pl.ds(q * cols, cols), :],
            (((1,), (1,)), ((), ())), preferred_element_type=jnp.float32,
        )
        parts[w + 4 * (g // 2), q, g % 2] = value.astype(jnp.bfloat16)

    def return_copy(w, q, h):
        return remote(parts.at[4 + w, q, h], parts.at[2 + w, q, h], ret_send.at[w, q, h], ret_recv.at[w, q, h], flip(4), z)

    def owner(e):
        y = 1 - y_bit if e & 2 else y_bit
        x = 1 - x_bit if e & 1 else x_bit
        return y * 2 + x

    def accumulate(e, q, h, slot):
        for part in (0, 1) if e < 2 else (h,):
            def body(i, carry):
                rows = pl.ds(pl.multiple_of(i * 64, 64), 64)
                value = parts[e, q, part, rows, :].astype(jnp.float32) + z_got[slot, q, part, rows, :].astype(jnp.float32)
                parts[e, q, part, rows, :] = value.astype(jnp.bfloat16)
                return carry
            lax.fori_loop(0, 2 * half // 64, body, 0)

    def right_copy(e, q, h):
        s = owner(e)
        src, dst = (parts.at[e, q], z_got.at[s + 1, q]) if e < 2 else (parts.at[e, q, h], z_got.at[s + 1, q, h])
        return remote(src, dst, z_send.at[e, q, h], z_recv.at[s + 1, q, h], me, lax.rem(z + 1, z_n))

    def left_copy(e, q, h):
        s = owner(e)
        src, dst = (parts.at[e, q], z_got.at[s, q]) if e < 2 else (parts.at[e, q, h], z_got.at[s, q, h])
        return remote(src, dst, z_send.at[e, q, h], z_recv.at[s, q, h], me, lax.rem(z + z_n - 1, z_n))

    def z_round(e, q, h, k):
        s = owner(e)
        if k < z_n:
            @pl.when((z == k - 1) & (z < s))
            def _():
                if k > 1:
                    right_copy(e, q, h).wait_recv()
                    accumulate(e, q, h, s + 1)
                right_copy(e, q, h).start()

            @pl.when((z == z_n - k) & (z > s))
            def _():
                if k > 1:
                    left_copy(e, q, h).wait_recv()
                    accumulate(e, q, h, s)
                left_copy(e, q, h).start()
        else:
            @pl.when(z == s)
            def _():
                @pl.when(z > 0)
                def _():
                    right_copy(e, q, h).wait_recv()
                    accumulate(e, q, h, s + 1)

                @pl.when(z < z_n - 1)
                def _():
                    left_copy(e, q, h).wait_recv()
                    accumulate(e, q, h, s)
                at = pl.ds(pl.multiple_of((core * CHUNKS + q) * cols, cols), cols)
                for part in (0, 1) if e < 2 else (h,):
                    fin_copy(e, q, part).start()
                    grad_ref[pl.ds(part * half, half), at] = parts[e, q, part, :half, :]

    def fin_copy(e, q, h):
        return remote(parts.at[e, q, h, pl.ds(half, half)], fin_got.at[q, h], fin_send.at[q, h], fin_recv.at[q, h], flip(1), z)

    def project():
        b = y_bit * 2 + core
        own = pl.ds(pl.multiple_of(b * high_rows, high_rows), high_rows)
        width = cols
        def body(i, carry):
            at = pl.ds(pl.multiple_of(i * width, width), width)
            value = 0.0
            for g in range(4):
                lanes = slice(g % 2 * half, (g % 2 + 1) * half)
                pair = (coords_ref[own, lanes], coords_got[0, :, lanes]) if g < 2 else (coords_got[1, :, lanes], coords_got[2, :, lanes])
                value = value + jnp.dot(
                    jnp.concatenate(pair, axis=1), cots[g, :, at], preferred_element_type=jnp.float32
                )
            proj[:, at] = value
            return carry
        lax.fori_loop(0, proj.shape[1] // width, body, 0)

    out_rows = proj.shape[0] // 2
    proj_copy = remote(proj_send, proj_got, px_send, px_recv, flip(2), z)

    def send_projected():
        project()
        there = pl.ds(pl.multiple_of((1 - x_bit) * out_rows, out_rows), out_rows)
        proj_send[...] = proj[there, :].astype(jnp.bfloat16)
        proj_copy.start()

    def sum_copy(m):
        return remote(sums.at[0], sums.at[m], s_send.at[m], s_recv.at[m], flip(m), z)

    def zsum_copy(step):
        return remote(zsums.at[0], zsums.at[step], t_send.at[step], t_recv.at[step], me, (z + step) % z_n)

    here = pl.ds(pl.multiple_of(x_bit * out_rows, out_rows), out_rows)

    def send_sums():
        proj_copy.wait()
        owned = proj[here, :] + proj_got[...].astype(jnp.float32)
        proj[here, :] = owned
        sums[0] = jnp.zeros((8, 128), jnp.float32) + jnp.sum(owned * owned)
        for m in range(1, 8):
            sum_copy(m).start()

    def send_zsums():
        for m in range(1, 8):
            sum_copy(m).wait()
        zsums[0] = jnp.sum(sums[...], axis=0)
        for step in range(1, z_n):
            zsum_copy(step).start()

    def dir_copy(m):
        return remote(dirs.at[me], dirs.at[me], d_send.at[m], d_recv.at[m], flip(m), z)

    def send_dirs():
        for step in range(1, z_n):
            zsum_copy(step).wait()
        total = jnp.sum(zsums[...], axis=0)
        factor = (1.0 / jnp.sqrt(total + norm_epsilon))[0:1, 0:1]
        one, two, direction = moments(factor, proj[here, :], first_ref[...], second_ref[...])
        new_first_ref[...] = one
        new_second_ref[...] = two
        dirs[me] = direction
        for m in range(1, 8):
            dir_copy(m).start()

    def take_dirs():
        for m in range(1, 8):
            dir_copy(m).wait()
        dirs_out_ref[...] = dirs[...].reshape(dirs_out_ref.shape)

    def take_weight(q):
        w_copy(q).wait()
        if q + AHEAD < CHUNKS:
            w_copy(q + AHEAD).start()
        for g in range(2):
            unit(g, 1, q)

    def own_units(q):
        if q == 0:
            for h in range(2):
                core_copy(h).wait()
        for g in range(2):
            unit(g, 0, q)

    taken = []

    def forwarded(h):
        if h not in taken:
            forward_copy(h).wait_recv()
            taken.append(h)

    for kind, *at in ORDER:
        if kind == START:
            y_copy(1).start()
        elif kind == OWN:
            own_units(*at)
        elif kind == X:
            take_weight(*at)
        elif kind == Y:
            y_copy(*at).wait()
            forward_copy(*at).start()
        elif kind == BACK:
            e, q, h = at
            forwarded(h)
            unit(2 + h, e - 2, q)
            return_copy(e - 2, q, h).start()
        elif kind == Z:
            e, q, h, k = at
            if e >= 2 and k == 1:
                return_copy(e - 2, q, h).wait()
            z_round(e, q, h, k)
        elif kind == PROJECT:
            for h in range(2):
                forwarded(h)
            for m in range(1, 4):
                coords_copy(m).wait()
            send_projected()
        else:
            {SUMS: send_sums, ZSUMS: send_zsums, DIRS: send_dirs}[kind]()
    take_dirs()
    for q in range(CHUNKS):
        for h in range(2):
            fin_copy(0, q, h).wait()
            at = pl.ds(pl.multiple_of(((1 - core) * CHUNKS + q) * cols, cols), cols)
            grad_ref[pl.ds(h * half, half), at] = fin_got[q, h]
    for h in range(2):
        forward_copy(h).wait_send()
    for e in range(4):
        @pl.when(z != owner(e))
        def _():
            for q in range(CHUNKS):
                for h in range(1 if e < 2 else 2):
                    right_copy(e, q, h).wait_send()


def exchange(z_n, cotangent, gate_weight, coords, first_moment, second_moment):
    tokens, hidden = cotangent.shape
    w_rows = gate_weight.shape[0]
    cols = w_rows // CHUNKS
    rank = coords.shape[0]
    own = first_moment.shape[0]
    vmem = pl.BlockSpec(memory_space=pltpu.VMEM)
    hbm = pl.BlockSpec(memory_space=pl.ANY)
    dma = pltpu.SemaphoreType.DMA
    bf16, f32 = jnp.bfloat16, jnp.float32
    flops = 2 * 4 * tokens * 2 * w_rows * hidden
    return pl.pallas_call(
        functools.partial(exchange_kernel, z_n),
        out_shape=[
            jax.ShapeDtypeStruct((tokens, 2 * w_rows), bf16),
            jax.ShapeDtypeStruct(first_moment.shape, f32),
            jax.ShapeDtypeStruct(first_moment.shape, f32),
            jax.ShapeDtypeStruct((rank, hidden), bf16),
        ],
        in_specs=[hbm, hbm, vmem, vmem, vmem],
        out_specs=[vmem] * 4,
        scratch_shapes=[
            pltpu.VMEM((4, tokens, hidden), bf16),
            pltpu.VMEM((2, w_rows, hidden), bf16),
            pltpu.VMEM((6, CHUNKS, 2, tokens, cols), bf16),
            pltpu.VMEM((z_n + 1, CHUNKS, 2, tokens, cols), bf16),
            pltpu.VMEM((CHUNKS, 2, tokens // 2, cols), bf16),
            pltpu.VMEM((3, rank // 4, tokens), bf16),
            pltpu.VMEM((2 * own, hidden), f32),
            pltpu.VMEM((own, hidden), bf16),
            pltpu.VMEM((own, hidden), bf16),
            pltpu.VMEM((8, 8, 128), f32),
            pltpu.VMEM((z_n, 8, 128), f32),
            pltpu.VMEM((8, own, hidden), bf16),
            dma((3,)),
            dma((6,)), dma((6,)),
            dma((CHUNKS,)), dma((CHUNKS,)),
            dma((2, CHUNKS, 2)), dma((2, CHUNKS, 2)),
            dma((4, CHUNKS, 2)), dma((z_n + 1, CHUNKS, 2)),
            dma((CHUNKS, 2)), dma((CHUNKS, 2)),
            dma((3,)), dma((3,)),
            dma, dma,
            dma((8,)), dma((8,)),
            dma((z_n,)), dma((z_n,)),
            dma((8,)), dma((8,)),
        ],
        compiler_params=pltpu.CompilerParams(
            collective_id=0, has_side_effects=True, vmem_limit_bytes=62 * 1024 * 1024
        ),
        cost_estimate=pl.CostEstimate(flops=flops, bytes_accessed=24000000, transcendentals=0),
    )(cotangent, gate_weight, coords, first_moment, second_moment)


def on_pairs(z_n, activations, cotangent, gate_weight, basis, first_moment, second_moment):
    own_rows = gate_weight.shape[0]
    tokens = activations.shape[0]
    rank = basis.shape[1]
    me = lax.axis_index("dp")
    coords = lax.dot_general(
        basis, activations, (((0,), (1,)), ((), ())), preferred_element_type=jnp.float32
    ).astype(jnp.bfloat16)
    coords = coords.reshape(2, 2, 2, rank // 8, tokens).transpose(0, 2, 1, 3, 4).reshape(rank, tokens)
    input_grad, new_first, new_second, direction = exchange(
        z_n, cotangent, gate_weight, coords, first_moment, second_moment
    )
    basis_rows = lax.dynamic_slice_in_dim(basis, me * own_rows, own_rows, 0)
    weight_step = jnp.dot(
        basis_rows, direction, preferred_element_type=jnp.float32
    ).astype(jnp.bfloat16)
    return (input_grad, weight_step, new_first, new_second)


def solution(mesh):
    dp_n, z_n = mesh.shape["dp"], mesh.shape["tensor"]
    assert dp_n == 2 * z_n and dp_n % 4 == 0
    paired = (dp_n, z_n) == (8, 4)
    body = functools.partial(on_pairs, z_n) if paired else functools.partial(on_device, dp_n, z_n)
    in_specs = (
        P("dp", None),
        P("dp", "tensor"),
        P("dp", "tensor"),
        P(),
        P("dp", "tensor"),
        P("dp", "tensor"),
    )
    out_specs = (P("dp", "tensor"), P("dp", "tensor"), P("dp", "tensor"), P("dp", "tensor"))
    return jax.shard_map(
        body,
        mesh=mesh,
        in_specs=in_specs,
        out_specs=out_specs,
        check_vma=False,
    )
```
